256 devices in a mesh: row: 16 (over z_lo, y), col: 16 (over x, z_hi, core).
Axes of the slice: x: 4, y: 4, z: 8 (z_hi: 2, z_lo: 4; z = z_hi * 4 + z_lo), core: 2. Of those that a mesh axis runs over, the one named last changes fastest.
Arguments:
- activations: bfloat16 [512, 28672], P('row', 'col'), may hold values from -6 to 6
- act_grads: bfloat16 [512, 8192], P('col', 'row'), may hold values from -1.5 to 1.5
- eigen_act: bfloat16 [28672, 28672], P('col', 'row'), may hold values from -0.03125 to 0.03125
- eigen_grad: bfloat16 [8192, 8192], P('row', 'col'), may hold values from -0.0625 to 0.0625
- example_ids: int32 [512], replicated, may hold values from 0 to 31, never falling along the last dimension, each value on 1 to 32 neighbouring positions
Outputs:
- lambda_out: float32 [8192, 28672], P('col', 'row')
The draws below stay inside these ranges and needn't reach their ends.
Inputs may be any that keep to these rules, and one draw needn't show every extreme that they name: `example_ids`: example ids never fall along the tokens; each example has 1 to 32 tokens and one has exactly 32.
All inputs are finite; a program needn't handle non-finite values.
Results may differ from the reference program's by a relative error of at most 0.0023.
Values may be sent and summed in bfloat16 or wider, within the bound.
No kernel may reach another device: no remote copies, remote signals or barrier semaphores. Data moves between devices by JAX's collectives and lax.ppermute only.
A program may use at most 64 MiB of HBM per device.

```python
import math
import jax
import jax.numpy as jnp
import numpy as np
from jax import lax

D = 8192
FF = 28672
TOKENS = 512
MOST_LEN = 32
EXAMPLES = 32


def steps_of(own_key, dims, split, smallest, high):
    gain, own = 1.0, jax.random.fold_in(own_key, 6)
    for dim, shards_of in split:
        steps = jnp.exp(jax.random.uniform(jax.random.fold_in(own, dim), (shards_of,), jnp.float32, smallest / len(split), high / len(split)))
        gain = gain * jnp.repeat(steps, dims[dim] // shards_of).reshape([-1 if axis == dim else 1 for axis in range(len(dims))])
    return gain


def split_up(number_of, total, bound, slope):
    weights = [(1 << 20) // math.isqrt(grade ** slope) + 1 for grade in range(2, number_of + 1)]
    rest, given = total - bound - (number_of - 1), [1] * (number_of - 1)
    while rest > 0:
        movable = [i for i in range(number_of - 1) if given[i] < bound]
        pool, left = sum([weights[i] for i in movable]), rest
        for i in movable:
            extra = min(bound - given[i], max(1, left * weights[i] // pool), rest)
            given[i] = given[i] + extra
            rest = rest - extra
    return np.array([bound] + given)


def ragged(own_key, number_of, total, bound, slope):
    if number_of == 2:
        one = jax.random.randint(own_key, (), max(1, total - bound), min(bound, total - 1) + 1)
        return jnp.stack([one, total - one])
    tallies = jnp.asarray(split_up(number_of, total, bound, slope), jnp.int32)
    couples = (number_of - 1) // 2
    giver, taker = tallies[1:1 + 2 * couples:2], tallies[2:2 + 2 * couples:2]
    room = jnp.minimum(giver - 1, bound - taker)
    moved = jax.random.randint(jax.random.fold_in(own_key, 1), (couples,), 0, 1 << 20) % (room + 1)
    tallies = tallies.at[1:1 + 2 * couples:2].set(giver - moved).at[2:2 + 2 * couples:2].set(taker + moved)
    return tallies[jax.random.permutation(jax.random.fold_in(own_key, 2), number_of)]


def centred(rng, shape, spread, reach, split=(), dtype=jnp.bfloat16):
    factor_of = steps_of(rng, shape, split, -0.22, 0.18) if split else 1.0
    drawn = jax.random.normal(rng, shape, jnp.float32) * spread * factor_of
    return jnp.minimum(jnp.maximum(drawn, -reach), reach).astype(dtype)


def setup_inputs(seed: int = 0) -> dict:
    key_list = jax.random.split(jax.random.key(seed), 6)
    return {
        "activations": centred(key_list[0], (TOKENS, FF), 1.0, 6.0, ((0, 16), (1, 16))),
        "act_grads": centred(key_list[1], (TOKENS, D), 0.25, 1.5, ((0, 16), (1, 16))),
        "eigen_act": centred(key_list[2], (FF, FF), FF ** -0.5, 0.03125, ((0, 16), (1, 16))),
        "eigen_grad": centred(key_list[3], (D, D), D ** -0.5, 0.0625, ((0, 16), (1, 16))),
        "example_ids": jnp.searchsorted(jnp.cumsum(ragged(key_list[4], EXAMPLES, TOKENS, MOST_LEN, 0)), jnp.arange(TOKENS), side="right").astype(jnp.int32),
    }


def example_slots(example_ids):
    total = example_ids.shape[0]
    numbers = jnp.arange(EXAMPLES).astype(jnp.int32)
    below = (example_ids[None, :] < numbers[:, None]).astype(jnp.int32)
    starts = jnp.sum(below, axis=1).astype(jnp.int32)
    positions = starts[:, None] + jnp.arange(MOST_LEN).astype(jnp.int32)[None, :]
    clipped = jnp.minimum(positions, total - 1).astype(jnp.int32)
    valid = (positions < total) & (example_ids[clipped] == numbers[:, None])
    return clipped, valid


def reference(activations, act_grads, eigen_act, eigen_grad, example_ids):
    act_rot = jnp.dot(activations, eigen_act, preferred_element_type=jnp.float32).astype(jnp.bfloat16)
    grad_rot = jnp.dot(act_grads, eigen_grad, preferred_element_type=jnp.float32).astype(jnp.bfloat16)
    slots, valid = example_slots(example_ids)

    def step(total, index):
        rows = slots[index]
        keep = valid[index][:, None]
        grad_rows = grad_rot[rows]
        act_rows = act_rot[rows]
        grad_rows = jnp.where(keep, grad_rows, jnp.zeros_like(grad_rows))
        act_rows = jnp.where(keep, act_rows, jnp.zeros_like(act_rows))
        block = jnp.dot(grad_rows.T, act_rows, preferred_element_type=jnp.float32)
        return total + block * block, None

    start = jnp.zeros((act_grads.shape[1], activations.shape[1]), jnp.float32)
    total, unused = lax.scan(step, start, jnp.arange(EXAMPLES).astype(jnp.int32))
    return total / EXAMPLES
```

```python
import jax
import jax.numpy as jnp
from jax import lax
from jax.sharding import Mesh, PartitionSpec as P

MOST_LEN = 32
ROW = ("zl", "y")
COL = ("x", "zh", "core")
F32 = jnp.float32
BF16 = jnp.bfloat16


def shifts(size, by):
    return [(i, (i + by) % size) for i in range(size)]


def swaps(size, by):
    return [(i, i ^ by) for i in range(size)]


def dot(a, b):
    return jnp.dot(a, b, preferred_element_type=F32)


def gather_grads(act_grads):
    pair = jnp.stack([act_grads, lax.ppermute(act_grads, "core", swaps(2, 1))])
    quad = jnp.stack([pair, lax.ppermute(pair, "zh", swaps(2, 1))])
    parts = [quad] + [lax.ppermute(quad, "x", shifts(4, s)) for s in (1, 2, 3)]
    return jnp.stack(parts).reshape(-1, act_grads.shape[1])


def grad_blocks(x, zh, core):
    return jnp.array(
        [((x - s) % 4) * 4 + (zh ^ h) * 2 + (core ^ c) for s in range(4) for h in range(2) for c in range(2)]
    )


def sum_grads(part, y, zl):
    blocks = part.reshape(4, 4, -1, part.shape[1])
    piece = lambda a, i: lax.dynamic_index_in_dim(a, i % 4, 0, False)
    total = piece(blocks, y)
    for s in (1, 2, 3):
        total = total + lax.ppermute(piece(blocks, y + s), "y", shifts(4, s))
    own = piece(total, zl)
    for s in (1, 2, 3):
        own = own + lax.ppermute(piece(total, zl ^ s), "zl", swaps(4, s))
    own = own.astype(BF16)
    line = jnp.stack([own] + [lax.ppermute(own, "zl", swaps(4, s)) for s in (1, 2, 3)])
    ring = jnp.stack([line] + [lax.ppermute(line, "y", shifts(4, s)) for s in (1, 2, 3)])
    return ring.reshape(-1, part.shape[1])


def local(activations, act_grads, eigen_act, eigen_grad, example_ids):
    zl, y, x, zh, core = (lax.axis_index(name) for name in ("zl", "y", "x", "zh", "core"))
    half = eigen_act.shape[1] // 2
    eigen_own = lax.dynamic_slice_in_dim(eigen_act, core * half, half, 1)
    eigen_other = lax.dynamic_slice_in_dim(eigen_act, (1 - core) * half, half, 1)

    with jax.named_scope("gather_line"):
        line = jnp.concatenate([activations] + [lax.ppermute(activations, "zl", swaps(4, s)) for s in (1, 2, 3)])
    with jax.named_scope("gather_grads"):
        grads = gather_grads(act_grads)

    pairs = []
    for s in (1, 2, 3, 0):
        with jax.named_scope("rotate"):
            route = [(j * 4 + i, (j + i + s) % 4 * 4 + i) for j in range(4) for i in range(4)]
            rows = lax.ppermute(line, ("y", "x"), route)
            away = dot(rows, eigen_other).astype(BF16)
            pair = dot(rows, eigen_own) + lax.ppermute(away, "core", swaps(2, 1)).astype(F32)
        with jax.named_scope("sum_ring"):
            pairs.append(lax.ppermute(pair.astype(BF16), "x", shifts(4, s)).astype(F32) if s else pair)
    with jax.named_scope("sum_far"):
        total = pairs[3] + pairs[0] + pairs[1] + pairs[2]
        total = total + lax.ppermute(total.astype(BF16), "zh", swaps(2, 1)).astype(F32)
        mine = total.astype(BF16)
    with jax.named_scope("gather_ring"):
        own = jnp.concatenate([mine] + [lax.ppermute(mine, "x", shifts(4, s)) for s in (1, 2, 3)])
        other = lax.ppermute(own, "core", swaps(2, 1))
        act_rot = jnp.concatenate([jnp.where(core == 0, own, other), jnp.where(core == 0, other, own)], axis=1)

    with jax.named_scope("sum_grads"):
        grad_rot = sum_grads(dot(grads, eigen_grad), y, zl)

    with jax.named_scope("slots"):
        tokens = example_ids.shape[0]
        examples = tokens // 16
        step = tokens // 16
        act_block = jnp.array([(zl ^ h) * 4 + (y - x + s) % 4 for s in range(4) for h in range(4)])
        blocks = grad_blocks(x, zh, core)
        grad_block = jnp.concatenate(
            [blocks[None, ((y - s) % 4) * 4 + (zl ^ h)] for s in range(4) for h in range(4)]
        )
        within = jnp.arange(step)
        act_token = (act_block[:, None] * step + within).reshape(-1)
        grad_token = (grad_block[:, None] * step + within).reshape(-1)
        bounds = jnp.sum(example_ids[None, :] < jnp.arange(examples + 1)[:, None], axis=1)
        slot = bounds[:-1, None] + jnp.arange(MOST_LEN)
        slot = jnp.where(slot < bounds[1:, None], slot, -1).reshape(-1, 1)
        take_act = (slot == act_token).astype(BF16)
        take_grad = (slot == grad_token).astype(BF16)
    with jax.named_scope("squares"):
        act_rows = dot(take_act, act_rot).astype(BF16).reshape(examples, MOST_LEN, -1)
        grad_rows = dot(take_grad, grad_rot).astype(BF16).reshape(examples, MOST_LEN, -1)
        blocks = jnp.einsum("eki,ekj->eij", grad_rows, act_rows, preferred_element_type=F32)
        return jnp.sum(blocks * blocks * (1 / examples), axis=0)


def solution(mesh):
    fine = Mesh(mesh.devices.reshape(4, 4, 4, 2, 2), ROW + COL)
    in_specs = (P(ROW, COL), P(COL, ROW), P(COL, ROW), P(ROW, COL), P())
    return jax.shard_map(local, mesh=fine, in_specs=in_specs, out_specs=P(COL, ROW), check_vma=False)
```

```python
import jax
import jax.numpy as jnp
from jax import lax
from jax.experimental import pallas as pl
from jax.experimental.pallas import tpu as pltpu
from jax.sharding import Mesh, PartitionSpec as P

MOST_LEN = 32
ROW = ("zl", "y")
COL = ("x", "zh", "core")
F32 = jnp.float32
BF16 = jnp.bfloat16


def shift(a, axis, by):
    return lax.ppermute(a, axis, [(i, (i + by) % 4) for i in range(4)])


def swap(a, axis, by=1):
    size = 2 if axis in ("zh", "core") else 4
    return lax.ppermute(a, axis, [(i, i ^ by) for i in range(size)])


def tie(*arrays):
    return lax.optimization_barrier(arrays)


def dot(a, b):
    return jnp.dot(a, b, preferred_element_type=F32)


def piece(a, i):
    return lax.dynamic_index_in_dim(a, i, 0, False)


def rotate_kernel(which_ref, rows_ref, eigen_ref, out_ref, sum_ref):
    step = pl.program_id(0)

    @pl.when(step == 0)
    def _():
        sum_ref[...] = dot(rows_ref[...], eigen_ref[...])

    @pl.when(step == 1)
    def _():
        out_ref[...] = (sum_ref[...] + dot(rows_ref[...], eigen_ref[...])).astype(out_ref.dtype)


def rotate(rows, eigen, which, dtype):
    tokens, depth = rows.shape
    half, deep = eigen.shape[1] // 2, depth // 2
    return pl.pallas_call(
        rotate_kernel,
        out_shape=jax.ShapeDtypeStruct((tokens, half), dtype),
        grid_spec=pltpu.PrefetchScalarGridSpec(
            num_scalar_prefetch=1,
            grid=(2,),
            in_specs=[
                pl.BlockSpec((tokens, deep), lambda k, w: (0, k)),
                pl.BlockSpec((deep, half), lambda k, w: (k, w[0])),
            ],
            out_specs=pl.BlockSpec((tokens, half), lambda k, w: (0, 0)),
            scratch_shapes=[pltpu.VMEM((tokens, half), F32)],
        ),
        compiler_params=pltpu.CompilerParams(vmem_limit_bytes=56 << 20),
        cost_estimate=pl.CostEstimate(flops=2 * tokens * depth * half, bytes_accessed=2 * depth * half, transcendentals=0),
        name="rotate",
    )(which.reshape(1), rows, eigen)


def local(activations, act_grads, eigen_act, eigen_grad, example_ids):
    zl, y, x, zh, core = (lax.axis_index(name) for name in ("zl", "y", "x", "zh", "core"))
    block = activations.shape[0]
    group = 4 * block

    with jax.named_scope("gather_line"):
        line = jnp.concatenate([activations, swap(activations, "zl", 1)])
        line = jnp.concatenate([line, swap(line, "zl", 2)])
    with jax.named_scope("gather_grads"):
        grads = jnp.concatenate([act_grads, swap(act_grads, "zh")])
        grads = jnp.concatenate([grads] + [shift(grads, "x", s) for s in (1, 2, 3)])
        grads = jnp.concatenate([grads, swap(grads, "core")])
    with jax.named_scope("sum_grads"):
        part = dot(grads, eigen_grad)
        line, part = tie(line, part)
        part = part + swap(part.astype(BF16), "zl", 2).astype(F32)
    with jax.named_scope("gather_plane"):
        ring = [line] + [shift(line, "y", s) for s in (1, 2, 3)]
        ring[1], ring[2], ring[3], part = tie(ring[1], ring[2], ring[3], part)
        tokens = jnp.concatenate(ring)
    with jax.named_scope("sum_grads"):
        part = part + swap(part.astype(BF16), "zl", 1).astype(F32)

    with jax.named_scope("rotate"):
        away = rotate(tokens, eigen_act, 1 - core, BF16)
        pair = rotate(tokens, eigen_act, core, F32) + swap(away, "core").astype(F32)
        pairs = [[pair.reshape(4, group, -1)]]
    totals = []
    for parts in pairs:
        with jax.named_scope("sum_ring"):
            at = lambda i: piece(parts[0], i % 4)
            total = at(x)
            for s in (1, 2, 3):
                total = total + shift(at(x + s).astype(BF16), "x", s).astype(F32)
        totals.append(total)
    totals[0], part = tie(totals[0], part)
    with jax.named_scope("sum_grads"):
        part = part + swap(part.astype(BF16), "y", 1).astype(F32)
    columns = []
    for total in totals:
        with jax.named_scope("sum_far"):
            mine = (total + swap(total.astype(BF16), "zh").astype(F32)).astype(BF16)
        if not columns:
            mine, part = tie(mine, part)
            with jax.named_scope("sum_grads"):
                grad_rot = (part + swap(part.astype(BF16), "y", 2).astype(F32)).astype(BF16)
        with jax.named_scope("gather_ring"):
            own = jnp.concatenate([mine] + [shift(mine, "x", s) for s in (1, 2, 3)])
            if not columns:
                own, grad_rot = tie(own, grad_rot)
            other = swap(own, "core")
            columns.append((jnp.where(core == 0, own, other), jnp.where(core == 0, other, own)))

    with jax.named_scope("slots"):
        examples = example_ids.shape[0] // 16
        row = lax.broadcasted_iota(jnp.int32, (1, example_ids.shape[0]), 1)
        within, outer, inner = row % block, row // group, row // block % 4
        act_token = ((zl ^ inner) * 4 + (y - x + outer) % 4) * block + within
        gathered = row // block
        from_x = (x - gathered // 2 % 4) % 4
        grad_token = (from_x * 4 + (zh ^ (gathered % 2)) * 2 + (core ^ (gathered // 8))) * block + within
        bounds = jnp.sum(example_ids[None, :] < jnp.arange(examples + 1)[:, None], axis=1)
        slot = bounds[:-1, None] + jnp.arange(MOST_LEN)
        slot = jnp.where(slot < bounds[1:, None], slot, -1).reshape(-1, 1)
        take_act = (slot == act_token).astype(BF16)
        take_grad = (slot == grad_token).astype(BF16)
    with jax.named_scope("squares"):
        grad_rows = dot(take_grad, grad_rot).astype(BF16).reshape(examples, MOST_LEN, -1)
        sums = [[], []]
        for two in columns:
            act_rows = dot(take_act, jnp.concatenate(two, axis=1)).astype(BF16).reshape(examples, MOST_LEN, -1)
            blocks = jnp.einsum("eki,ekj->eij", grad_rows, act_rows, preferred_element_type=F32)
            squares = jnp.sum(blocks * blocks * (1 / examples), axis=0)
            sums[0].append(squares[:, : two[0].shape[1]])
            sums[1].append(squares[:, two[0].shape[1] :])
        return jnp.concatenate(sums[0] + sums[1], axis=1)


def solution(mesh):
    fine = Mesh(mesh.devices.reshape(4, 4, 4, 2, 2), ROW + COL)
    in_specs = (P(ROW, COL), P(COL, ROW), P(COL, ROW), P(ROW, COL), P())
    return jax.shard_map(local, mesh=fine, in_specs=in_specs, out_specs=P(COL, ROW), check_vma=False)
```

```python
import jax
import jax.numpy as jnp
from jax import lax
from jax.sharding import Mesh, PartitionSpec as P

MOST_LEN = 32
ROW = ("zl", "y")
COL = ("x", "zh", "core")
F32 = jnp.float32
BF16 = jnp.bfloat16


def shift(a, axis, by):
    return lax.ppermute(a, axis, [(i, (i + by) % 4) for i in range(4)])


def swap(a, axis, by=1):
    size = 2 if axis in ("zh", "core") else 4
    return lax.ppermute(a, axis, [(i, i ^ by) for i in range(size)])


def tie(*arrays):
    return lax.optimization_barrier(arrays)


def dot(a, b):
    return jnp.dot(a, b, preferred_element_type=F32)


def piece(a, i):
    return lax.dynamic_index_in_dim(a, i, 0, False)


def local(activations, act_grads, eigen_act, eigen_grad, example_ids):
    zl, y, x, zh, core = (lax.axis_index(name) for name in ("zl", "y", "x", "zh", "core"))
    block = activations.shape[0]
    group = 4 * block
    chunks = (512, eigen_act.shape[1] // 2 - 512)

    with jax.named_scope("gather_line"):
        line = jnp.concatenate([activations] + [swap(activations, "zl", s) for s in (1, 2, 3)])
    with jax.named_scope("gather_grads"):
        grads = jnp.concatenate([act_grads, swap(act_grads, "zh")])
        line, grads = tie(line, grads)

    with jax.named_scope("gather_plane"):
        ring = [line] + [shift(line, "y", s) for s in (1, 2, 3)]
    with jax.named_scope("gather_grads"):
        grads = jnp.concatenate([grads] + [shift(grads, "x", s) for s in (1, 2, 3)])
        ring[1], ring[2], ring[3], grads = tie(ring[1], ring[2], ring[3], grads)
        grads = jnp.concatenate([grads, swap(grads, "core")])
    with jax.named_scope("gather_plane"):
        tokens = jnp.concatenate(ring)

    with jax.named_scope("sum_grads"):
        part = dot(grads, eigen_grad).reshape(2, 2 * group, -1)
        sums = piece(part, y % 2) + swap(piece(part, 1 - y % 2).astype(BF16), "y", 1).astype(F32)
        sums = sums.reshape(2, group, -1)
        sums = piece(sums, y // 2) + swap(piece(sums, 1 - y // 2), "y", 2).astype(F32)

    pairs = []
    lo = 0
    for wide in chunks:
        with jax.named_scope("rotate"):
            eigen_own = lax.dynamic_slice_in_dim(eigen_act, lo + core * wide, wide, 1)
            eigen_away = lax.dynamic_slice_in_dim(eigen_act, lo + (1 - core) * wide, wide, 1)
            away = dot(tokens, eigen_away).astype(BF16)
            pair = dot(tokens, eigen_own) + swap(away, "core").astype(F32)
            pairs.append([pair.reshape(4, group, wide)])
        lo += 2 * wide
    pairs = [pairs[0] + pairs[1]]
    totals = []
    for parts in pairs:
        with jax.named_scope("sum_ring"):
            at = lambda i: jnp.concatenate([piece(p, i % 4) for p in parts], axis=1)
            total = at(x)
            for s in (1, 2, 3):
                total = total + shift(at(x + s).astype(BF16), "x", s).astype(F32)
        totals.append(total)
    totals[0], sums = tie(totals[0], sums)
    with jax.named_scope("sum_grads"):
        sums = sums + swap(sums.astype(BF16), "zl", 1).astype(F32)
        sums = sums + swap(sums.astype(BF16), "zl", 2).astype(F32)
        grad_rot = sums.astype(BF16)
    columns = []
    for total in totals:
        with jax.named_scope("sum_far"):
            mine = (total + swap(total.astype(BF16), "zh").astype(F32)).astype(BF16)
        if not columns:
            mine, grad_rot = tie(mine, grad_rot)
            with jax.named_scope("sum_grads"):
                grad_rot = jnp.concatenate([grad_rot, swap(grad_rot, "y", 2)])
                grad_rot = jnp.concatenate([grad_rot, swap(grad_rot, "y", 1)])
        with jax.named_scope("gather_ring"):
            own = jnp.concatenate([mine] + [shift(mine, "x", s) for s in (1, 2, 3)])
            if not columns:
                own, grad_rot = tie(own, grad_rot)
            other = swap(own, "core")
            lower, upper = jnp.where(core == 0, own, other), jnp.where(core == 0, other, own)
            cuts = chunks if own.shape[1] == sum(chunks) else (own.shape[1],)
            at = 0
            both = []
            for wide in cuts:
                both += [lower[:, at : at + wide], upper[:, at : at + wide]]
                at += wide
            columns.append(jnp.concatenate(both, axis=1))

    with jax.named_scope("slots"):
        examples = example_ids.shape[0] // 16
        row = lax.broadcasted_iota(jnp.int32, (1, example_ids.shape[0]), 1)
        within, outer, inner = row % block, row // group, row // block % 4
        act_token = ((zl ^ inner) * 4 + (y - x + outer) % 4) * block + within
        gathered = ((y % 2) ^ (row // (2 * group))) * 8 + ((y // 2) ^ (outer % 2)) * 4 + inner
        from_x = (x - gathered // 2 % 4) % 4
        grad_token = (from_x * 4 + (zh ^ (gathered % 2)) * 2 + (core ^ (gathered // 8))) * block + within
        bounds = jnp.sum(example_ids[None, :] < jnp.arange(examples + 1)[:, None], axis=1)
        slot = bounds[:-1, None] + jnp.arange(MOST_LEN)
        slot = jnp.where(slot < bounds[1:, None], slot, -1).reshape(-1, 1)
        take_act = (slot == act_token).astype(BF16)
        take_grad = (slot == grad_token).astype(BF16)
    with jax.named_scope("squares"):
        grad_rows = dot(take_grad, grad_rot).astype(BF16).reshape(examples, MOST_LEN, -1)
        sums = []
        for act_rot in columns:
            act_rows = dot(take_act, act_rot).astype(BF16).reshape(examples, MOST_LEN, -1)
            blocks = jnp.einsum("eki,ekj->eij", grad_rows, act_rows, preferred_element_type=F32)
            sums.append(jnp.sum(blocks * blocks * (1 / examples), axis=0))
        return sums[0]


def solution(mesh):
    fine = Mesh(mesh.devices.reshape(4, 4, 4, 2, 2), ROW + COL)
    in_specs = (P(ROW, COL), P(COL, ROW), P(COL, ROW), P(ROW, COL), P())
    return jax.shard_map(local, mesh=fine, in_specs=in_specs, out_specs=P(COL, ROW), check_vma=False)
```

```python
import jax
import jax.numpy as jnp
from jax import lax
from jax.sharding import Mesh, PartitionSpec as P

MOST_LEN = 32
ROW = ("zl", "y")
COL = ("x", "zh", "core")
F32 = jnp.float32
BF16 = jnp.bfloat16


def shift(a, axis, by):
    return lax.ppermute(a, axis, [(i, (i + by) % 4) for i in range(4)])


def swap(a, axis, by=1):
    size = 2 if axis in ("zh", "core") else 4
    return lax.ppermute(a, axis, [(i, i ^ by) for i in range(size)])


def tie(*arrays):
    return lax.optimization_barrier(arrays)


def dot(a, b):
    return jnp.dot(a, b, preferred_element_type=F32)


def piece(a, i):
    return lax.dynamic_index_in_dim(a, i, 0, False)


def local(activations, act_grads, eigen_act, eigen_grad, example_ids):
    zl, y, x, zh, core = (lax.axis_index(name) for name in ("zl", "y", "x", "zh", "core"))
    block = activations.shape[0]
    group = 4 * block
    chunks = (512, eigen_act.shape[1] // 2 - 512)

    with jax.named_scope("gather_line"):
        line = jnp.concatenate([activations] + [swap(activations, "zl", s) for s in (1, 2, 3)])
    with jax.named_scope("gather_grads"):
        grads = jnp.concatenate([act_grads, swap(act_grads, "zh")])
        line, grads = tie(line, grads)

    with jax.named_scope("gather_plane"):
        ring = [line] + [shift(line, "y", s) for s in (1, 2, 3)]
    with jax.named_scope("gather_grads"):
        grads = jnp.concatenate([grads] + [shift(grads, "x", s) for s in (1, 2, 3)])
        ring[1], ring[2], ring[3], grads = tie(ring[1], ring[2], ring[3], grads)
        grads = jnp.concatenate([grads, swap(grads, "core")])
    with jax.named_scope("gather_plane"):
        tokens = jnp.concatenate(ring)

    with jax.named_scope("sum_grads"):
        part = dot(grads, eigen_grad).reshape(2, 2 * group, -1)
        sums = piece(part, y % 2) + swap(piece(part, 1 - y % 2).astype(BF16), "y", 1).astype(F32)
        sums = sums.reshape(2, group, -1)
        sums = piece(sums, y // 2) + swap(piece(sums, 1 - y // 2), "y", 2).astype(F32)

    pairs = []
    lo = 0
    for wide in chunks:
        with jax.named_scope("rotate"):
            eigen_own = lax.dynamic_slice_in_dim(eigen_act, lo + core * wide, wide, 1)
            eigen_away = lax.dynamic_slice_in_dim(eigen_act, lo + (1 - core) * wide, wide, 1)
            away = dot(tokens, eigen_away).astype(BF16)
            pair = dot(tokens, eigen_own) + swap(away, "core").astype(F32)
            pairs.append([pair.reshape(4, group, wide)])
        lo += 2 * wide
    pairs = [pairs[0] + pairs[1]]
    totals = []
    for parts in pairs:
        with jax.named_scope("sum_ring"):
            at = lambda i: jnp.concatenate([piece(p, i % 4) for p in parts], axis=1)
            total = at(x)
            for s in (1, 2, 3):
                total = total + shift(at(x + s).astype(BF16), "x", s).astype(F32)
        totals.append(total)
    totals[0], sums = tie(totals[0], sums)
    with jax.named_scope("sum_grads"):
        sums = sums + swap(sums.astype(BF16), "zl", 1).astype(F32)
    columns = []
    for total in totals:
        with jax.named_scope("sum_far"):
            mine = (total + swap(total.astype(BF16), "zh").astype(F32)).astype(BF16)
        if not columns:
            mine, sums = tie(mine, sums)
            with jax.named_scope("sum_grads"):
                part = (sums + swap(sums.astype(BF16), "zl", 2).astype(F32)).astype(BF16)
                grad_rot = jnp.concatenate([part] + [shift(part, "y", s) for s in (1, 2, 3)])
        with jax.named_scope("gather_ring"):
            own = jnp.concatenate([mine] + [shift(mine, "x", s) for s in (1, 2, 3)])
            if not columns:
                own, grad_rot = tie(own, grad_rot)
            other = swap(own, "core")
            lower, upper = jnp.where(core == 0, own, other), jnp.where(core == 0, other, own)
            cuts = chunks if own.shape[1] == sum(chunks) else (own.shape[1],)
            at = 0
            both = []
            for wide in cuts:
                both += [lower[:, at : at + wide], upper[:, at : at + wide]]
                at += wide
            columns.append(jnp.concatenate(both, axis=1))

    with jax.named_scope("slots"):
        examples = example_ids.shape[0] // 16
        row = lax.broadcasted_iota(jnp.int32, (1, example_ids.shape[0]), 1)
        within, outer, inner = row % block, row // group, row // block % 4
        act_token = ((zl ^ inner) * 4 + (y - x + outer) % 4) * block + within
        owner = (y - outer) % 4
        gathered = owner % 2 * 8 + owner // 2 * 4 + inner
        from_x = (x - gathered // 2 % 4) % 4
        grad_token = (from_x * 4 + (zh ^ (gathered % 2)) * 2 + (core ^ (gathered // 8))) * block + within
        bounds = jnp.sum(example_ids[None, :] < jnp.arange(examples + 1)[:, None], axis=1)
        slot = bounds[:-1, None] + jnp.arange(MOST_LEN)
        slot = jnp.where(slot < bounds[1:, None], slot, -1).reshape(-1, 1)
        take_act = (slot == act_token).astype(BF16)
        take_grad = (slot == grad_token).astype(BF16)
    with jax.named_scope("squares"):
        grad_rows = dot(take_grad, grad_rot).astype(BF16).reshape(examples, MOST_LEN, -1)
        sums = []
        for act_rot in columns:
            act_rows = dot(take_act, act_rot).astype(BF16).reshape(examples, MOST_LEN, -1)
            blocks = jnp.einsum("eki,ekj->eij", grad_rows, act_rows, preferred_element_type=F32)
            sums.append(jnp.sum(blocks * blocks * (1 / examples), axis=0))
        return sums[0]


def solution(mesh):
    fine = Mesh(mesh.devices.reshape(4, 4, 4, 2, 2), ROW + COL)
    in_specs = (P(ROW, COL), P(COL, ROW), P(COL, ROW), P(ROW, COL), P())
    return jax.shard_map(local, mesh=fine, in_specs=in_specs, out_specs=P(COL, ROW), check_vma=False)
```

```python
import jax
import jax.numpy as jnp
from jax import lax
from jax.sharding import Mesh, PartitionSpec as P

MOST_LEN = 32
ROW = ("zl", "y")
COL = ("x", "zh", "core")
F32 = jnp.float32
BF16 = jnp.bfloat16


def shift(a, axis, by):
    return lax.ppermute(a, axis, [(i, (i + by) % 4) for i in range(4)])


def swap(a, axis, by=1):
    size = 2 if axis in ("zh", "core") else 4
    return lax.ppermute(a, axis, [(i, i ^ by) for i in range(size)])


def tie(*arrays):
    return lax.optimization_barrier(arrays)


def dot(a, b):
    return jnp.dot(a, b, preferred_element_type=F32)


def piece(a, i):
    return lax.dynamic_index_in_dim(a, i, 0, False)


def local(activations, act_grads, eigen_act, eigen_grad, example_ids):
    zl, y, x, zh, core = (lax.axis_index(name) for name in ("zl", "y", "x", "zh", "core"))
    block = activations.shape[0]
    group = 4 * block
    chunks = (512, eigen_act.shape[1] // 2 - 512)

    with jax.named_scope("gather_line"):
        line = jnp.concatenate([activations] + [swap(activations, "zl", s) for s in (1, 2, 3)])
    with jax.named_scope("gather_grads"):
        grads = jnp.concatenate([act_grads, swap(act_grads, "zh")])
        line, grads = tie(line, grads)

    with jax.named_scope("gather_plane"):
        ring = [line] + [shift(line, "y", s) for s in (1, 2, 3)]
    with jax.named_scope("gather_grads"):
        grads = jnp.concatenate([grads] + [shift(grads, "x", s) for s in (1, 2, 3)])
        parts = []
        for lo, wide in ((0, chunks[0]), (2 * chunks[0], chunks[1])):
            parts += [lax.dynamic_slice_in_dim(eigen_act, lo + side * wide, wide, 1) for side in (core, 1 - core)]
        ring[1], ring[2], ring[3], grads, *parts = tie(ring[1], ring[2], ring[3], grads, *parts)
        grads = jnp.concatenate([grads, swap(grads, "core")])
    with jax.named_scope("gather_plane"):
        tokens = jnp.concatenate(ring)

    with jax.named_scope("sum_grads"):
        part = dot(grads, eigen_grad).reshape(2, 2 * group, -1)
        sums = piece(part, y % 2) + swap(piece(part, 1 - y % 2).astype(BF16), "y", 1).astype(F32)
        sums = sums.reshape(2, group, -1)
        sums = piece(sums, y // 2) + swap(piece(sums, 1 - y // 2), "y", 2).astype(F32)

    pairs = []
    lo = 0
    for wide in chunks:
        with jax.named_scope("rotate"):
            eigen_own, eigen_away = parts[:2] if lo == 0 else parts[2:]
            away = dot(tokens, eigen_away).astype(BF16)
            pair = dot(tokens, eigen_own) + swap(away, "core").astype(F32)
            pairs.append([pair.reshape(4, group, wide)])
        lo += 2 * wide
    pairs = [pairs[0] + pairs[1]]
    totals = []
    for parts in pairs:
        with jax.named_scope("sum_ring"):
            at = lambda i: jnp.concatenate([piece(p, i % 4) for p in parts], axis=1)
            total = at(x)
            for s in (1, 2, 3):
                total = total + shift(at(x + s).astype(BF16), "x", s).astype(F32)
        totals.append(total)
    totals[0], sums = tie(totals[0], sums)
    with jax.named_scope("sum_grads"):
        sums = sums + swap(sums.astype(BF16), "zl", 1).astype(F32)
    columns = []
    for total in totals:
        with jax.named_scope("sum_far"):
            mine = (total + swap(total.astype(BF16), "zh").astype(F32)).astype(BF16)
        if not columns:
            mine, sums = tie(mine, sums)
            with jax.named_scope("sum_grads"):
                part = (sums + swap(sums.astype(BF16), "zl", 2).astype(F32)).astype(BF16)
                grad_rot = jnp.concatenate([part] + [shift(part, "y", s) for s in (1, 2, 3)])
        with jax.named_scope("gather_ring"):
            own = jnp.concatenate([mine] + [shift(mine, "x", s) for s in (1, 2, 3)])
            if not columns:
                own, grad_rot = tie(own, grad_rot)
            other = swap(own, "core")
            lower, upper = jnp.where(core == 0, own, other), jnp.where(core == 0, other, own)
            cuts = chunks if own.shape[1] == sum(chunks) else (own.shape[1],)
            at = 0
            both = []
            for wide in cuts:
                both += [lower[:, at : at + wide], upper[:, at : at + wide]]
                at += wide
            columns.append(jnp.concatenate(both, axis=1))

    with jax.named_scope("slots"):
        examples = example_ids.shape[0] // 16
        row = lax.broadcasted_iota(jnp.int32, (1, example_ids.shape[0]), 1)
        within, outer, inner = row % block, row // group, row // block % 4
        act_token = ((zl ^ inner) * 4 + (y - x + outer) % 4) * block + within
        owner = (y - outer) % 4
        gathered = owner % 2 * 8 + owner // 2 * 4 + inner
        from_x = (x - gathered // 2 % 4) % 4
        grad_token = (from_x * 4 + (zh ^ (gathered % 2)) * 2 + (core ^ (gathered // 8))) * block + within
        bounds = jnp.sum(example_ids[None, :] < jnp.arange(examples + 1)[:, None], axis=1)
        slot = bounds[:-1, None] + jnp.arange(MOST_LEN)
        slot = jnp.where(slot < bounds[1:, None], slot, -1).reshape(-1, 1)
        take_act = (slot == act_token).astype(BF16)
        take_grad = (slot == grad_token).astype(BF16)
    with jax.named_scope("squares"):
        grad_rows = dot(take_grad, grad_rot).astype(BF16).reshape(examples, MOST_LEN, -1)
        sums = []
        for act_rot in columns:
            act_rows = dot(take_act, act_rot).astype(BF16).reshape(examples, MOST_LEN, -1)
            blocks = jnp.einsum("eki,ekj->eij", grad_rows, act_rows, preferred_element_type=F32)
            sums.append(jnp.sum(blocks * blocks * (1 / examples), axis=0))
        return sums[0]


def solution(mesh):
    fine = Mesh(mesh.devices.reshape(4, 4, 4, 2, 2), ROW + COL)
    in_specs = (P(ROW, COL), P(COL, ROW), P(COL, ROW), P(ROW, COL), P())
    return jax.shard_map(local, mesh=fine, in_specs=in_specs, out_specs=P(COL, ROW), check_vma=False)
```
